32 devices in a mesh: parts: 2 (over x), frame: 16 (over z, y, core).
Axes of the slice: x: 2, y: 2, z: 4, core: 2. Of those that a mesh axis runs over, the one named last changes fastest.
Arguments:
- latent: bfloat16 [32, 32, 64, 512], P(('parts', 'frame')), parts along dimension 0, may hold values from -6 to 6
- column_project: bfloat16 [512, 1536], replicated, may hold values from -0.25 to 0.25
- column_output: bfloat16 [512, 512], replicated, may hold values from -0.25 to 0.25
- row_query_key_value: bfloat16 [512, 1536], replicated, may hold values from -0.25 to 0.25
- row_output: bfloat16 [512, 512], replicated, may hold values from -0.25 to 0.25
- frame_project: bfloat16 [512, 1536], replicated, may hold values from -0.25 to 0.25
- frame_output: bfloat16 [512, 512], replicated, may hold values from -0.25 to 0.25
- expand_weight: bfloat16 [512, 2048], replicated, may hold values from -0.25 to 0.25
- contract_weight: bfloat16 [2048, 512], replicated, may hold values from -0.125 to 0.125
Outputs:
- result: bfloat16 [32, 32, 64, 512], P(('parts', 'frame')), parts along dimension 0
The draws below stay inside these ranges and needn't reach their ends.
There are 2 independent parts, one for each index of `parts`. The reference program is written for one: setup_inputs(seed, part) draws one part's arguments, and reference() takes and returns one part's arrays. A program takes and returns all parts, laid end to end along the dimension named above; an argument that names none is the same for every part. Nothing has to cross between parts.
All inputs are finite; a program needn't handle non-finite values.
Results may differ from the reference program's by a relative error of at most 0.014.
Values may be sent and summed in bfloat16 or wider, within the bound.
No kernel may reach another device: no remote copies, remote signals or barrier semaphores. Data moves between devices by JAX's collectives and lax.ppermute only.
A program may use at most 128 MiB of HBM per device.

```python
import math
import jax
import jax.numpy as jnp
from jax import lax

D = 512
HEADS = 8
FFN = 2048
H = 32
W = 64
F = 16


def block_scale(stream_key, extent, pieces, least, high):
    gain = 1.0
    for position, parts in pieces:
        heights = jax.random.uniform(jax.random.fold_in(jax.random.fold_in(stream_key, 6), position), (parts,), jnp.float32, least / len(pieces), high / len(pieces))
        gain = gain * jnp.repeat(jnp.exp(heights), extent[position] // parts).reshape((-1,) + (1,) * (len(extent) - 1 - position))
    return gain


def noise(rng, shape, scale, most, pieces=(), dtype=jnp.bfloat16):
    level = block_scale(rng, shape, pieces, -0.22, 0.18) if pieces else 1.0
    array = jax.random.normal(rng, shape, jnp.float32) * scale * level
    return jnp.minimum(jnp.maximum(array, -most), most).astype(dtype)


def setup_inputs(seed: int = 0, part: int = 0) -> dict:
    key_of = jax.random.split(jax.random.key(seed), 10)
    part_splits = jax.random.split(jax.random.fold_in(key_of[9], part), 10)
    latent = noise(part_splits[0], (F, H, W, D), 1.0, 6.0, ((0, 16),))
    column_project = noise(key_of[1], (D, 3 * D), D ** -0.5, 0.25)
    column_output = noise(key_of[2], (D, D), D ** -0.5, 0.25)
    row_query_key_value = noise(key_of[3], (D, 3 * D), D ** -0.5, 0.25)
    row_output = noise(key_of[4], (D, D), D ** -0.5, 0.25)
    frame_project = noise(key_of[5], (D, 3 * D), D ** -0.5, 0.25)
    frame_output = noise(key_of[6], (D, D), D ** -0.5, 0.25)
    expand_weight = noise(key_of[7], (D, FFN), D ** -0.5, 0.25)
    contract_weight = noise(key_of[8], (FFN, D), FFN ** -0.5, 0.125)
    return dict(latent=latent, column_project=column_project, column_output=column_output, row_query_key_value=row_query_key_value, row_output=row_output, frame_project=frame_project, frame_output=frame_output, expand_weight=expand_weight, contract_weight=contract_weight)


EPS_NORM = 1e-05
EPS_HEAD = 1e-06

def layer_normalize(stream):
    values = stream.astype(jnp.float32)
    centre = values - lax.optimization_barrier(jnp.mean(values, axis=-1, keepdims=True))
    spread = lax.optimization_barrier(jnp.mean(centre * centre, axis=-1, keepdims=True))
    return (centre * lax.rsqrt(spread + EPS_NORM)).astype(jnp.bfloat16)

def head_norm(block, heads):
    reshaped_input = block.reshape(block.shape[:-1] + (heads, block.shape[-1] // heads))
    scaled = reshaped_input * lax.rsqrt(lax.optimization_barrier(jnp.mean(reshaped_input * reshaped_input, axis=-1, keepdims=True)) + EPS_HEAD)
    return scaled.reshape(block.shape).astype(jnp.bfloat16)

def project(normed, weight, heads):
    width = normed.shape[-1]
    joined = jnp.dot(normed.reshape(-1, width), weight, preferred_element_type=jnp.float32)
    joined = joined.reshape(normed.shape[:-1] + (3 * width,))
    queries = head_norm(joined[..., :width], heads)
    key_block = head_norm(joined[..., width:2 * width], heads)
    value_block = joined[..., 2 * width:].astype(jnp.bfloat16)
    return (queries, key_block, value_block)

def attend_core(queries, key_block, value_block, axis, heads):
    width = queries.shape[-1]
    head_dimension_size = width // heads
    reshaped_input = []
    for block in (queries, key_block, value_block):
        moved = jnp.moveaxis(block, axis, -2)
        reshaped_input.append(moved.reshape(moved.shape[:-1] + (heads, head_dimension_size)).astype(jnp.float32))
    attention_logits = jnp.einsum('...irp,...vrp->...riv', reshaped_input[0], reshaped_input[1]) / math.sqrt(head_dimension_size)
    expd = jnp.exp(attention_logits)
    attention_weights = (expd / lax.optimization_barrier(jnp.sum(expd, axis=-1, keepdims=True))).astype(jnp.bfloat16)
    blended_values = jnp.einsum('...jki,...ijt->...kjt', attention_weights.astype(jnp.float32), reshaped_input[2]).astype(jnp.bfloat16)
    blended_values = blended_values.reshape(blended_values.shape[:-2] + (width,))
    return jnp.moveaxis(blended_values, -2, axis)

def finish(stream, blended_values, weight):
    width = stream.shape[-1]
    added = jnp.dot(blended_values.reshape(-1, width), weight, preferred_element_type=jnp.float32)
    return (stream.astype(jnp.float32) + added.reshape(stream.shape)).astype(jnp.bfloat16)

def sublayer(stream, weight_in, weight_out, axis, heads):
    queries, key_block, value_block = project(layer_normalize(stream), weight_in, heads)
    return finish(stream, attend_core(queries, key_block, value_block, axis, heads), weight_out)

def feed_forward(stream, weight_in, weight_out):
    width = stream.shape[-1]
    normed = layer_normalize(stream).reshape(-1, width)
    hidden = jax.nn.gelu(jnp.dot(normed, weight_in, preferred_element_type=jnp.float32)).astype(jnp.bfloat16)
    added = jnp.dot(hidden, weight_out, preferred_element_type=jnp.float32)
    return (stream.astype(jnp.float32) + added.reshape(stream.shape)).astype(jnp.bfloat16)

def reference(latent, column_project, column_output, row_query_key_value, row_output, frame_project, frame_output, expand_weight, contract_weight):
    stream = sublayer(latent, column_project, column_output, 1, HEADS)
    stream = sublayer(stream, row_query_key_value, row_output, 2, HEADS)
    stream = sublayer(stream, frame_project, frame_output, 0, HEADS)
    return feed_forward(stream, expand_weight, contract_weight)
```

```python
import functools

import jax
import jax.numpy as jnp
from jax import lax
from jax.experimental import pallas as pl
from jax.experimental.pallas import tpu as pltpu
from jax.sharding import PartitionSpec as P

HEADS = 8
EPS_NORM = 1e-05
EPS_HEAD = 1e-06
BF = jnp.bfloat16
F32 = jnp.float32
SIDE = 16
GROUP = 64


def dot(a, b):
    return jnp.dot(a, b, preferred_element_type=F32)


def dot_nt(a, b):
    return lax.dot_general(a, b, (((1,), (1,)), ((), ())), preferred_element_type=F32)


def iota(shape, dim):
    return lax.broadcasted_iota(jnp.int32, shape, dim)


def swap_matrix():
    n = SIDE * SIDE
    r, c = iota((n, n), 0), iota((n, n), 1)
    hit = (r // SIDE == c % SIDE) & (r % SIDE == c // SIDE)
    return jnp.where(hit, 1.0, 0.0).astype(BF)


def head_blocks(head, value):
    n = 4 * head
    same = iota((n, n), 0) // head == iota((n, n), 1) // head
    return jnp.where(same, value, 0.0).astype(BF)


def layer_normalize(x):
    v = x.astype(F32)
    centre = v - jnp.mean(v, axis=-1, keepdims=True)
    spread = jnp.mean(centre * centre, axis=-1, keepdims=True)
    return (centre * lax.rsqrt(spread + EPS_NORM)).astype(BF)


def head_norm(block, averager, scale):
    half = averager.shape[0]
    squares = (block * block).astype(BF)
    out = []
    for c in range(0, block.shape[1], half):
        mean = dot(squares[:, c : c + half], averager)
        out.append((block[:, c : c + half] * (lax.rsqrt(mean + EPS_HEAD) * scale)).astype(BF))
    return out


def spread_heads(block, head):
    lane = iota(block.shape, 1) // head
    zero = jnp.zeros_like(block)
    return jnp.concatenate([jnp.where(lane == h, block, zero) for h in range(4)], axis=0)


def sublayer(x, project_ref, output_ref, line):
    tokens, width = x.shape
    head = width // HEADS
    half = 4 * head
    averager = head_blocks(head, 1.0 / head)
    summer = head_blocks(head, 1.0)
    normed = layer_normalize(x)
    queries = head_norm(dot(normed, project_ref[:, :width]), averager, head**-0.5)
    keys = head_norm(dot(normed, project_ref[:, width : 2 * width]), averager, 1.0)
    values = dot(normed, project_ref[:, 2 * width :]).astype(BF)
    rows = []
    for s in range(0, tokens, GROUP):
        parts = []
        for c in range(width // half):
            q = queries[c][s : s + GROUP]
            k = spread_heads(keys[c][s : s + GROUP], head)
            v = spread_heads(values[s : s + GROUP, c * half : (c + 1) * half], head)
            e = jnp.exp(dot_nt(q, k))
            if line < GROUP:
                own = iota(e.shape, 0) // line == (iota(e.shape, 1) % GROUP) // line
                e = jnp.where(own, e, 0.0)
            e = e.astype(BF)
            parts.append((dot(e, v) / dot(e, summer)).astype(BF))
        rows.append(jnp.concatenate(parts, axis=1))
    mixed = jnp.concatenate(rows, axis=0)
    return (x.astype(F32) + dot(mixed, output_ref[...])).astype(BF)


def to_lines(x, swap):
    length, side, width = x.shape
    parts = []
    for a in range(0, length, SIDE):
        tile = x[a : a + SIDE].reshape(SIDE * side, width)
        parts.append(dot(swap, tile).astype(BF).reshape(side, SIDE, width))
    return jnp.concatenate(parts, axis=1).reshape(side * length, width)


def from_lines(x, swap, length):
    width = x.shape[1]
    x = x.reshape(SIDE, length, width)
    parts = []
    for a in range(0, length, SIDE):
        tile = x[:, a : a + SIDE].reshape(SIDE * SIDE, width)
        parts.append(dot(swap, tile).astype(BF).reshape(SIDE, SIDE, width))
    return jnp.concatenate(parts, axis=0)


def feed_forward(x, expand_ref, contract_ref):
    hidden = expand_ref.shape[1]
    piece = 512
    normed = layer_normalize(x)
    total = x.astype(F32)
    for c in range(0, hidden, piece):
        h = jax.nn.gelu(dot(normed, expand_ref[:, c : c + piece])).astype(BF)
        total = total + dot(h, contract_ref[c : c + piece])
    return total.astype(BF)


def column_row_kernel(x_ref, cp_ref, co_ref, rp_ref, ro_ref, out_ref, mid_ref):
    rows, columns, width = x_ref.shape
    swap = swap_matrix()

    @pl.loop(0, columns // SIDE)
    def _(g):
        at = pl.ds(pl.multiple_of(g * SIDE, SIDE), SIDE)
        x = to_lines(x_ref[:, at, :], swap)
        y = sublayer(x, cp_ref, co_ref, rows)
        mid_ref[:, at, :] = from_lines(y, swap, rows)

    step = 512 // columns

    @pl.loop(0, rows // step)
    def _(g):
        at = pl.ds(g * step, step)
        x = mid_ref[at].reshape(step * columns, width)
        out_ref[at] = sublayer(x, rp_ref, ro_ref, columns).reshape(step, columns, width)


def frame_kernel(x_ref, fp_ref, fo_ref, we_ref, wc_ref, out_ref):
    frames, pixels, width = x_ref.shape
    swap = swap_matrix()

    @pl.loop(0, pixels // SIDE)
    def _(g):
        at = pl.ds(pl.multiple_of(g * SIDE, SIDE), SIDE)
        x = to_lines(x_ref[:, at, :], swap)
        y = sublayer(x, fp_ref, fo_ref, frames)
        y = feed_forward(y, we_ref, wc_ref)
        out_ref[:, at, :] = from_lines(y, swap, frames)


VMEM = pl.BlockSpec(memory_space=pltpu.VMEM)


def local_call(kernel, out_shape, args, flops, scratch=()):
    size = sum(a.size * 2 for a in args)
    return pl.pallas_call(
        kernel,
        out_shape=out_shape,
        in_specs=[VMEM] * len(args),
        out_specs=jax.tree.map(lambda _: VMEM, out_shape),
        scratch_shapes=list(scratch),
        cost_estimate=pl.CostEstimate(flops=flops, bytes_accessed=size, transcendentals=0),
        compiler_params=pltpu.CompilerParams(vmem_limit_bytes=56 * 2**20),
    )(*args)


def per_device(latent, cp, co, rp, ro, fp, fo, we, wc):
    _, rows, columns, width = latent.shape
    owners = lax.axis_size("frame")
    share = rows * columns // owners
    stream = local_call(
        column_row_kernel,
        jax.ShapeDtypeStruct((rows, columns, width), BF),
        (latent[0], cp, co, rp, ro),
        2 * rows * columns * width * width * 8,
        [pltpu.VMEM((rows, columns, width), BF)],
    )
    stream = stream.reshape(owners, share, width)
    stream = lax.all_to_all(stream, "frame", split_axis=0, concat_axis=0, tiled=True)
    stream = local_call(
        frame_kernel,
        jax.ShapeDtypeStruct((owners, share, width), BF),
        (stream, fp, fo, we, wc),
        2 * rows * columns * width * width * 12,
    )
    stream = lax.all_to_all(stream, "frame", split_axis=0, concat_axis=0, tiled=True)
    return stream.reshape(latent.shape)


def solution(mesh):
    placed = (P(("parts", "frame"), None, None, None),) + (P(),) * 8
    return jax.shard_map(
        per_device,
        mesh=mesh,
        in_specs=placed,
        out_specs=P(("parts", "frame"), None, None, None),
        check_vma=False,
    )
```

```python
import functools
import math

import jax
import jax.numpy as jnp
from jax import lax
from jax.experimental import pallas as pl
from jax.experimental.pallas import tpu as pltpu
from jax.sharding import PartitionSpec as P

HEADS = 8
EPS_NORM = 1e-05
EPS_HEAD = 1e-06
BF = jnp.bfloat16
F32 = jnp.float32
SIDE = 16
GROUP = 64


def dot(a, b):
    return jnp.dot(a, b, preferred_element_type=F32)


def dot_nt(a, b):
    return lax.dot_general(a, b, (((1,), (1,)), ((), ())), preferred_element_type=F32)


def iota(shape, dim):
    return lax.broadcasted_iota(jnp.int32, shape, dim)


def swap_matrix():
    n = SIDE * SIDE
    r, c = iota((n, n), 0), iota((n, n), 1)
    hit = (r // SIDE == c % SIDE) & (r % SIDE == c // SIDE)
    return jnp.where(hit, 1.0, 0.0).astype(BF)


def head_blocks(head, value):
    n = 4 * head
    same = iota((n, n), 0) // head == iota((n, n), 1) // head
    return jnp.where(same, value, 0.0).astype(BF)


def layer_normalize(x):
    v = x.astype(F32)
    centre = v - jnp.mean(v, axis=-1, keepdims=True)
    spread = jnp.mean(centre * centre, axis=-1, keepdims=True)
    return (centre * lax.rsqrt(spread + EPS_NORM)).astype(BF)


def head_norm(block, averager, scale):
    half = averager.shape[0]
    squares = (block * block).astype(BF)
    out = []
    for c in range(0, block.shape[1], half):
        mean = dot(squares[:, c : c + half], averager)
        out.append((block[:, c : c + half] * (lax.rsqrt(mean + EPS_HEAD) * scale)).astype(BF))
    return out


def spread_heads(block, head):
    lane = iota(block.shape, 1) // head
    zero = jnp.zeros_like(block)
    return jnp.concatenate([jnp.where(lane == h, block, zero) for h in range(4)], axis=0)


def sublayer(x, project_ref, output_ref, line):
    tokens, width = x.shape
    head = width // HEADS
    half = 4 * head
    averager = head_blocks(head, 1.0 / head)
    summer = head_blocks(head, 1.0)
    normed = layer_normalize(x)
    queries = head_norm(dot(normed, project_ref[:, :width]), averager, head**-0.5)
    keys = head_norm(dot(normed, project_ref[:, width : 2 * width]), averager, 1.0)
    values = dot(normed, project_ref[:, 2 * width :]).astype(BF)
    rows = []
    for s in range(0, tokens, GROUP):
        parts = []
        for c in range(width // half):
            q = queries[c][s : s + GROUP]
            k = spread_heads(keys[c][s : s + GROUP], head)
            v = spread_heads(values[s : s + GROUP, c * half : (c + 1) * half], head)
            e = jnp.exp(dot_nt(q, k))
            if line < GROUP:
                own = iota(e.shape, 0) // line == (iota(e.shape, 1) % GROUP) // line
                e = jnp.where(own, e, 0.0)
            e = e.astype(BF)
            parts.append((dot(e, v) / dot(e, summer)).astype(BF))
        rows.append(jnp.concatenate(parts, axis=1))
    mixed = jnp.concatenate(rows, axis=0)
    return (x.astype(F32) + dot(mixed, output_ref[...])).astype(BF)


def to_lines(x, swap):
    length, side, width = x.shape
    parts = []
    for a in range(0, length, SIDE):
        tile = x[a : a + SIDE].reshape(SIDE * side, width)
        parts.append(dot(swap, tile).astype(BF).reshape(side, SIDE, width))
    return jnp.concatenate(parts, axis=1).reshape(side * length, width)


def from_lines(x, swap, length):
    width = x.shape[1]
    x = x.reshape(SIDE, length, width)
    parts = []
    for a in range(0, length, SIDE):
        tile = x[:, a : a + SIDE].reshape(SIDE * SIDE, width)
        parts.append(dot(swap, tile).astype(BF).reshape(SIDE, SIDE, width))
    return jnp.concatenate(parts, axis=0)


def feed_forward(x, expand_ref, contract_ref):
    hidden = expand_ref.shape[1]
    piece = 512
    normed = layer_normalize(x)
    total = x.astype(F32)
    for c in range(0, hidden, piece):
        h = jax.nn.gelu(dot(normed, expand_ref[:, c : c + piece])).astype(BF)
        total = total + dot(h, contract_ref[c : c + piece])
    return total.astype(BF)


def columns_of(x_ref, project_ref, output_ref, mid_ref):
    rows, columns, _ = x_ref.shape
    swap = swap_matrix()

    @pl.loop(0, columns // SIDE)
    def _(g):
        at = pl.ds(pl.multiple_of(g * SIDE, SIDE), SIDE)
        x = to_lines(x_ref[:, at, :], swap)
        y = sublayer(x, project_ref, output_ref, rows)
        mid_ref[:, at, :] = from_lines(y, swap, rows)


def rows_of(mid_ref, first, project_ref, output_ref, out_ref):
    rows, columns, width = out_ref.shape
    step = math.gcd(rows, 512 // columns)

    @pl.loop(0, rows // step)
    def _(g):
        x = mid_ref[pl.ds(first + g * step, step)].reshape(step * columns, width)
        y = sublayer(x, project_ref, output_ref, columns)
        out_ref[pl.ds(g * step, step)] = y.reshape(step, columns, width)


def column_row_kernel(x_ref, cp_ref, co_ref, rp_ref, ro_ref, mid_ref, out_ref):
    columns_of(x_ref, cp_ref, co_ref, mid_ref)
    rows_of(mid_ref, 0, rp_ref, ro_ref, out_ref)


def row_kernel(first, mid_ref, rp_ref, ro_ref, out_ref):
    rows_of(mid_ref, first, rp_ref, ro_ref, out_ref)


def frame_kernel(x_ref, fp_ref, fo_ref, we_ref, wc_ref, *rest):
    out_ref = rest[-1]
    frames, pixels, _ = x_ref.shape
    swap = swap_matrix()

    @pl.loop(0, pixels // SIDE)
    def _(g):
        at = pl.ds(pl.multiple_of(g * SIDE, SIDE), SIDE)
        x = to_lines(x_ref[:, at, :], swap)
        y = sublayer(x, fp_ref, fo_ref, frames)
        y = feed_forward(y, we_ref, wc_ref)
        out_ref[:, at, :] = from_lines(y, swap, frames)


VMEM = pl.BlockSpec(memory_space=pltpu.VMEM)


def local_call(kernel, out_shape, args, flops, scratch=(), after=()):
    size = sum(a.size * 2 for a in args)
    return pl.pallas_call(
        kernel,
        out_shape=out_shape,
        in_specs=[VMEM] * len(args) + [pl.BlockSpec(memory_space=pl.ANY)] * len(after),
        out_specs=jax.tree.map(lambda _: VMEM, out_shape),
        scratch_shapes=list(scratch),
        cost_estimate=pl.CostEstimate(flops=flops, bytes_accessed=size, transcendentals=0),
        compiler_params=pltpu.CompilerParams(vmem_limit_bytes=56 * 2**20),
    )(*args, *after)


def like(*shape):
    return jax.ShapeDtypeStruct(shape, BF)


CHUNKS = 2


def exchange(blocks):
    return lax.all_to_all(blocks, "frame", split_axis=0, concat_axis=0, tiled=True)


def per_device(latent, cp, co, rp, ro, fp, fo, we, wc):
    _, rows, columns, width = latent.shape
    owners = lax.axis_size("frame")
    height = rows // CHUNKS
    share = height * columns // owners
    unit = 2 * columns * width * width
    mid, first = local_call(
        column_row_kernel,
        (like(rows, columns, width), like(height, columns, width)),
        (latent[0], cp, co, rp, ro),
        unit * 4 * (rows + height),
    )
    chunks = [first] + [
        local_call(
            functools.partial(row_kernel, i * height),
            like(height, columns, width),
            (mid, rp, ro),
            unit * 4 * height,
        )
        for i in range(1, CHUNKS)
    ]
    owned = [exchange(chunk.reshape(owners, share, width)) for chunk in chunks]
    done = [
        local_call(
            frame_kernel,
            like(owners, share, width),
            (block, fp, fo, we, wc),
            unit * 12 * height,
            after=chunks[-1:] if i < CHUNKS - 1 else (),
        )
        for i, block in enumerate(owned)
    ]
    home = [exchange(block).reshape(height, columns, width) for block in done]
    return jnp.concatenate(home, axis=0)[None]


def solution(mesh):
    placed = (P(("parts", "frame"), None, None, None),) + (P(),) * 8
    return jax.shard_map(
        per_device,
        mesh=mesh,
        in_specs=placed,
        out_specs=P(("parts", "frame"), None, None, None),
        check_vma=False,
    )
```

```python
import functools
import math

import jax
import jax.numpy as jnp
from jax import lax
from jax.experimental import pallas as pl
from jax.experimental.pallas import tpu as pltpu
from jax.sharding import PartitionSpec as P

HEADS = 8
EPS_NORM = 1e-05
EPS_HEAD = 1e-06
BF = jnp.bfloat16
F32 = jnp.float32
SIDE = 16
SPAN = 128
FIRST = 2


def dot(a, b):
    return jnp.dot(a, b, preferred_element_type=F32)


def dot_nt(a, b):
    return lax.dot_general(a, b, (((1,), (1,)), ((), ())), preferred_element_type=F32)


def iota(shape, dim):
    return lax.broadcasted_iota(jnp.int32, shape, dim)


def swap_matrix():
    n = SIDE * SIDE
    r, c = iota((n, n), 0), iota((n, n), 1)
    hit = (r // SIDE == c % SIDE) & (r % SIDE == c // SIDE)
    return jnp.where(hit, 1.0, 0.0).astype(BF)


def head_blocks(head, value):
    n = 4 * head
    same = iota((n, n), 0) // head == iota((n, n), 1) // head
    return jnp.where(same, value, 0.0).astype(BF)


def layer_normalize(x):
    v = x.astype(F32)
    centre = v - jnp.mean(v, axis=-1, keepdims=True)
    spread = jnp.mean(centre * centre, axis=-1, keepdims=True)
    return (centre * lax.rsqrt(spread + EPS_NORM)).astype(BF)


def head_norm(block, averager, scale):
    half = averager.shape[0]
    squares = (block * block).astype(BF)
    out = []
    for c in range(0, block.shape[1], half):
        mean = dot(squares[:, c : c + half], averager)
        out.append((block[:, c : c + half] * (lax.rsqrt(mean + EPS_HEAD) * scale)).astype(BF))
    return out


def sublayer(x, project_ref, output_ref, line):
    tokens, width = x.shape
    head = width // HEADS
    half = 4 * head
    averager = head_blocks(head, 1.0 / head)
    normed = layer_normalize(x)
    queries = head_norm(dot(normed, project_ref[:, :width]), averager, head**-0.5)
    keys = head_norm(dot(normed, project_ref[:, width : 2 * width]), averager, 1.0)
    values = dot(normed, project_ref[:, 2 * width :]).astype(BF)
    span = SPAN
    pair = 2 * head
    own = iota((span, 2 * span), 0) // line == (iota((span, 2 * span), 1) % span) // line
    first = iota((span, pair), 1) < head
    ones = jnp.where((iota((2 * span, pair), 0) < span) == (iota((2 * span, pair), 1) < head), 1.0, 0.0).astype(BF)

    def spread(block):
        zero = jnp.zeros_like(block)
        return jnp.concatenate([jnp.where(first, block, zero), jnp.where(first, zero, block)], axis=0)

    rows = []
    for s in range(0, tokens, span):
        parts = []
        for h in range(0, width, pair):
            c, o = h // half, h % half
            q = queries[c][s : s + span, o : o + pair]
            k = spread(keys[c][s : s + span, o : o + pair])
            v = spread(values[s : s + span, h : h + pair])
            e = jnp.where(own, jnp.exp(dot_nt(q, k)), 0.0).astype(BF)
            r = dot(e, jnp.concatenate([v, ones], axis=1))
            parts.append((r[:, :pair] / r[:, pair:]).astype(BF))
        rows.append(jnp.concatenate(parts, axis=1))
    mixed = jnp.concatenate(rows, axis=0)
    return (x.astype(F32) + dot(mixed, output_ref[...])).astype(BF)


def to_lines(x, swap):
    length, side, width = x.shape
    parts = []
    for a in range(0, length, SIDE):
        tile = x[a : a + SIDE].reshape(SIDE * side, width)
        parts.append(dot(swap, tile).astype(BF).reshape(side, SIDE, width))
    return jnp.concatenate(parts, axis=1).reshape(side * length, width)


def from_lines(x, swap, length):
    width = x.shape[1]
    x = x.reshape(SIDE, length, width)
    parts = []
    for a in range(0, length, SIDE):
        tile = x[:, a : a + SIDE].reshape(SIDE * SIDE, width)
        parts.append(dot(swap, tile).astype(BF).reshape(SIDE, SIDE, width))
    return jnp.concatenate(parts, axis=0)


def feed_forward(x, expand_ref, contract_ref):
    hidden = expand_ref.shape[1]
    piece = 256
    normed = layer_normalize(x)
    total = x.astype(F32)
    for c in range(0, hidden, piece):
        h = jax.nn.gelu(dot(normed, expand_ref[:, c : c + piece])).astype(BF)
        total = total + dot(h, contract_ref[c : c + piece])
    return total.astype(BF)


def like(*shape):
    return jax.ShapeDtypeStruct(shape, BF)


VMEM = pl.BlockSpec(memory_space=pltpu.VMEM)
ANY = pl.BlockSpec(memory_space=pl.ANY)


def local_call(kernel, out_shape, args, specs, flops, scratch=()):
    size = sum(a.size * 2 for a in args)
    return pl.pallas_call(
        kernel,
        out_shape=out_shape,
        in_specs=specs,
        out_specs=jax.tree.map(lambda _: VMEM, out_shape),
        scratch_shapes=list(scratch),
        cost_estimate=pl.CostEstimate(flops=flops, bytes_accessed=size, transcendentals=0),
        compiler_params=pltpu.CompilerParams(vmem_limit_bytes=56 * 2**20),
    )(*args)


def rows_of(mid_ref, first, project_ref, output_ref, out_ref):
    rows, columns, width = out_ref.shape
    step = math.gcd(rows, 512 // columns)

    @pl.loop(0, rows // step)
    def _(g):
        x = mid_ref[pl.ds(first + g * step, step)].reshape(step * columns, width)
        y = sublayer(x, project_ref, output_ref, columns)
        out_ref[pl.ds(g * step, step)] = y.reshape(step, columns, width)


def column_row_kernel(x_ref, cp_ref, co_ref, rp_ref, ro_ref, mid_ref, out_ref):
    rows, columns, _ = x_ref.shape
    swap = swap_matrix()

    @pl.loop(0, columns // SIDE)
    def _(g):
        at = pl.ds(pl.multiple_of(g * SIDE, SIDE), SIDE)
        x = to_lines(x_ref[:, at, :], swap)
        y = sublayer(x, cp_ref, co_ref, rows)
        mid_ref[:, at, :] = from_lines(y, swap, rows)

    rows_of(mid_ref, 0, rp_ref, ro_ref, out_ref)


def row_kernel(first, mid_ref, rp_ref, ro_ref, out_ref):
    rows_of(mid_ref, first, rp_ref, ro_ref, out_ref)


def frame_kernel(x_ref, fp_ref, fo_ref, we_ref, wc_ref, *rest):
    out_ref = rest[-1]
    frames, pixels, _ = x_ref.shape
    swap = swap_matrix()
    size = frames * SIDE
    tiles = math.gcd(pixels // SIDE, max(1, 512 // size))

    @pl.loop(0, pixels // (tiles * SIDE))
    def _(t):
        at = [pl.ds(pl.multiple_of((t * tiles + i) * SIDE, SIDE), SIDE) for i in range(tiles)]
        x = jnp.concatenate([to_lines(x_ref[:, a, :], swap) for a in at], axis=0)
        y = sublayer(x, fp_ref, fo_ref, frames)
        y = feed_forward(y, we_ref, wc_ref)
        for i, a in enumerate(at):
            out_ref[:, a, :] = from_lines(y[i * size : (i + 1) * size], swap, frames)


def exchange(blocks):
    return lax.all_to_all(blocks, "frame", split_axis=0, concat_axis=0, tiled=True)


def per_device(latent, cp, co, rp, ro, fp, fo, we, wc):
    _, rows, columns, width = latent.shape
    owners = lax.axis_size("frame")
    unit = 2 * columns * width * width
    one = rows // FIRST
    two = rows - one
    mid, chunk_one = local_call(
        column_row_kernel,
        (like(rows, columns, width), like(one, columns, width)),
        (latent[0], cp, co, rp, ro),
        [VMEM] * 5,
        unit * 4 * (rows + one),
    )
    chunk_two = local_call(
        functools.partial(row_kernel, one),
        like(two, columns, width),
        (mid, rp, ro),
        [VMEM] * 3,
        unit * 4 * two,
    )
    home = []
    for chunk, after in ((chunk_one, (chunk_two,)), (chunk_two, ())):
        height = chunk.shape[0]
        share = height * columns // owners
        owned = exchange(chunk.reshape(owners, share, width))
        done = local_call(
            frame_kernel,
            like(owners, share, width),
            (owned, fp, fo, we, wc, *after),
            [VMEM] * 5 + [ANY] * len(after),
            unit * 12 * height,
        )
        home.append(exchange(done).reshape(height, columns, width))
    return jnp.concatenate(home, axis=0)[None]


def solution(mesh):
    placed = (P(("parts", "frame"), None, None, None),) + (P(),) * 8
    return jax.shard_map(
        per_device,
        mesh=mesh,
        in_specs=placed,
        out_specs=P(("parts", "frame"), None, None, None),
        check_vma=False,
    )
```

```python
import functools
import math

import jax
import jax.numpy as jnp
from jax import lax
from jax.experimental import pallas as pl
from jax.experimental.pallas import tpu as pltpu
from jax.sharding import PartitionSpec as P

HEADS = 8
EPS_NORM = 1e-05
EPS_HEAD = 1e-06
BF = jnp.bfloat16
F32 = jnp.float32
SIDE = 16
SPAN = 128
CHUNKS = 2


def dot(a, b):
    return jnp.dot(a, b, preferred_element_type=F32)


def dot_nt(a, b):
    return lax.dot_general(a, b, (((1,), (1,)), ((), ())), preferred_element_type=F32)


def iota(shape, dim):
    return lax.broadcasted_iota(jnp.int32, shape, dim)


def swap_matrix():
    n = SIDE * SIDE
    r, c = iota((n, n), 0), iota((n, n), 1)
    hit = (r // SIDE == c % SIDE) & (r % SIDE == c // SIDE)
    return jnp.where(hit, 1.0, 0.0).astype(BF)


def head_blocks(head, value):
    n = 4 * head
    same = iota((n, n), 0) // head == iota((n, n), 1) // head
    return jnp.where(same, value, 0.0).astype(BF)


def layer_normalize(x):
    v = x.astype(F32)
    centre = v - jnp.mean(v, axis=-1, keepdims=True)
    spread = jnp.mean(centre * centre, axis=-1, keepdims=True)
    return (centre * lax.rsqrt(spread + EPS_NORM)).astype(BF)


def head_norm(block, averager, eps):
    half = averager.shape[0]
    squares = (block * block).astype(BF)
    out = []
    for c in range(0, block.shape[1], half):
        mean = dot(squares[:, c : c + half], averager)
        out.append((block[:, c : c + half] * lax.rsqrt(mean + eps)).astype(BF))
    return out


def sublayer(x, project_ref, output_ref, line, first=0, count=None):
    tokens, width = x.shape
    count = count or line
    head = width // HEADS
    half = 4 * head
    normed = layer_normalize(x)

    def picked(block):
        if count == line:
            return block
        return block.reshape(tokens // line, line, width)[:, first : first + count].reshape(-1, width)

    queries = head_norm(dot(picked(normed), project_ref[:, :width]), head_blocks(head, 1.0), head * EPS_HEAD)
    keys = head_norm(dot(normed, project_ref[:, width : 2 * width]), head_blocks(head, 1.0 / head), EPS_HEAD)
    values = dot(normed, project_ref[:, 2 * width :]).astype(BF)
    span = SPAN
    asks = span // line * count
    pair = 2 * head
    own = iota((asks, 2 * span), 0) // count == (iota((asks, 2 * span), 1) % span) // line
    left = iota((span, pair), 1) < head
    ones = jnp.where((iota((2 * span, pair), 0) < span) == (iota((2 * span, pair), 1) < head), 1.0, 0.0).astype(BF)

    def spread(block):
        zero = jnp.zeros_like(block)
        return jnp.concatenate([jnp.where(left, block, zero), jnp.where(left, zero, block)], axis=0)

    rows = []
    for i, s in enumerate(range(0, tokens, span)):
        parts = []
        for h in range(0, width, pair):
            c, o = h // half, h % half
            q = queries[c][i * asks : (i + 1) * asks, o : o + pair]
            k = spread(keys[c][s : s + span, o : o + pair])
            v = spread(values[s : s + span, h : h + pair])
            e = jnp.where(own, jnp.exp(dot_nt(q, k)), 0.0).astype(BF)
            r = dot(e, jnp.concatenate([v, ones], axis=1))
            parts.append((r[:, :pair] / r[:, pair:]).astype(BF))
        rows.append(jnp.concatenate(parts, axis=1))
    mixed = jnp.concatenate(rows, axis=0)
    return (picked(x).astype(F32) + dot(mixed, output_ref[...])).astype(BF)


def to_lines(x, swap):
    length, side, width = x.shape
    parts = []
    for a in range(0, length, SIDE):
        tile = x[a : a + SIDE].reshape(SIDE * side, width)
        parts.append(dot(swap, tile).astype(BF).reshape(side, SIDE, width))
    return jnp.concatenate(parts, axis=1).reshape(side * length, width)


def from_lines(x, swap, length):
    width = x.shape[1]
    x = x.reshape(SIDE, length, width)
    parts = []
    for a in range(0, length, SIDE):
        tile = x[:, a : a + SIDE].reshape(SIDE * SIDE, width)
        parts.append(dot(swap, tile).astype(BF).reshape(SIDE, SIDE, width))
    return jnp.concatenate(parts, axis=0)


def feed_forward(x, expand_ref, contract_ref):
    hidden = expand_ref.shape[1]
    piece = 256
    normed = layer_normalize(x)
    total = x.astype(F32)
    for c in range(0, hidden, piece):
        h = jax.nn.gelu(dot(normed, expand_ref[:, c : c + piece])).astype(BF)
        total = total + dot(h, contract_ref[c : c + piece])
    return total.astype(BF)


def like(*shape):
    return jax.ShapeDtypeStruct(shape, BF)


VMEM = pl.BlockSpec(memory_space=pltpu.VMEM)
ANY = pl.BlockSpec(memory_space=pl.ANY)


def local_call(kernel, out_shape, args, specs, flops, scratch=(), out_spec=VMEM):
    size = sum(a.size * 2 for a in args)
    return pl.pallas_call(
        kernel,
        out_shape=out_shape,
        in_specs=specs,
        out_specs=jax.tree.map(lambda _: out_spec, out_shape),
        scratch_shapes=list(scratch),
        cost_estimate=pl.CostEstimate(flops=flops, bytes_accessed=size, transcendentals=0),
        compiler_params=pltpu.CompilerParams(vmem_limit_bytes=56 * 2**20),
    )(*args)


def column_row_kernel(first, x_hbm, cp_hbm, co_hbm, rp_hbm, ro_hbm, out_hbm, *scratch):
    x_ref, cp_ref, co_ref, rp_ref, ro_ref, mid_ref, out_ref, sems = scratch
    rows, columns, width = x_hbm.shape
    groups = columns // SIDE
    count = out_hbm.shape[0]
    step = math.gcd(count, 512 // columns)

    def at(g):
        return pl.ds(pl.multiple_of(g * SIDE, SIDE), SIDE)

    def fetch(g):
        return pltpu.make_async_copy(x_hbm.at[:, at(g), :], x_ref.at[g], sems.at[g])

    pairs = ((cp_hbm, cp_ref), (co_hbm, co_ref), (rp_hbm, rp_ref), (ro_hbm, ro_ref))
    weights = [pltpu.make_async_copy(h, v, sems.at[groups + i]) for i, (h, v) in enumerate(pairs)]
    fetch(0).start()
    weights[0].start()
    weights[1].start()
    for g in range(1, groups):
        fetch(g).start()
    weights[2].start()
    weights[3].start()
    swap = swap_matrix()
    weights[0].wait()
    weights[1].wait()

    @pl.loop(0, groups)
    def _(g):
        fetch(g).wait()
        y = sublayer(to_lines(x_ref[g], swap), cp_ref, co_ref, rows, first, count)
        mid_ref[:, at(g), :] = from_lines(y, swap, count)

    weights[2].wait()
    weights[3].wait()

    def give(g):
        part = pl.ds(g * step, step)
        return pltpu.make_async_copy(out_ref.at[part], out_hbm.at[part], sems.at[groups + 4])

    @pl.loop(0, count // step)
    def _(g):
        x = mid_ref[pl.ds(g * step, step)].reshape(step * columns, width)
        y = sublayer(x, rp_ref, ro_ref, columns)

        @pl.when(g > 0)
        def _():
            give(g - 1).wait()

        out_ref[pl.ds(g * step, step)] = y.reshape(step, columns, width)
        give(g).start()

    give(count // step - 1).wait()


def frame_kernel(x_ref, fp_ref, fo_ref, we_ref, wc_ref, *rest):
    out_ref = rest[-1]
    frames, pixels, _ = x_ref.shape
    swap = swap_matrix()
    size = frames * SIDE
    tiles = math.gcd(pixels // SIDE, max(1, 512 // size))

    @pl.loop(0, pixels // (tiles * SIDE))
    def _(t):
        at = [pl.ds(pl.multiple_of((t * tiles + i) * SIDE, SIDE), SIDE) for i in range(tiles)]
        x = jnp.concatenate([to_lines(x_ref[:, a, :], swap) for a in at], axis=0)
        y = sublayer(x, fp_ref, fo_ref, frames)
        y = feed_forward(y, we_ref, wc_ref)
        for i, a in enumerate(at):
            out_ref[:, a, :] = from_lines(y[i * size : (i + 1) * size], swap, frames)


def exchange(blocks):
    return lax.all_to_all(blocks, "frame", split_axis=0, concat_axis=0, tiled=True)


def per_device(latent, cp, co, rp, ro, fp, fo, we, wc):
    _, rows, columns, width = latent.shape
    owners = lax.axis_size("frame")
    unit = 2 * columns * width * width
    count = rows // CHUNKS
    chunks = [
        local_call(
            functools.partial(column_row_kernel, first),
            like(count, columns, width),
            (latent[0], cp, co, rp, ro),
            [ANY] * 5,
            unit * (2 * rows + 6 * count),
            [pltpu.VMEM((columns // SIDE, rows, SIDE, width), BF)]
            + [pltpu.VMEM(w.shape, BF) for w in (cp, co, rp, ro)]
            + [pltpu.VMEM((count, columns, width), BF)] * 2
            + [pltpu.SemaphoreType.DMA((columns // SIDE + 5,))],
            ANY,
        )
        for first in range(0, rows, count)
    ]
    home = []
    for chunk, after in zip(chunks, [chunks[1:2]] + [()] * CHUNKS):
        height = chunk.shape[0]
        share = height * columns // owners
        owned = exchange(chunk.reshape(owners, share, width))
        done = local_call(
            frame_kernel,
            like(owners, share, width),
            (owned, fp, fo, we, wc, *after),
            [VMEM] * 5 + [ANY] * len(after),
            unit * 12 * height,
        )
        home.append(exchange(done).reshape(height, columns, width))
    return jnp.concatenate(home, axis=0)[None]


def solution(mesh):
    placed = (P(("parts", "frame"), None, None, None),) + (P(),) * 8
    return jax.shard_map(
        per_device,
        mesh=mesh,
        in_specs=placed,
        out_specs=P(("parts", "frame"), None, None, None),
        check_vma=False,
    )
```

```python
import functools
import math

import jax
import jax.numpy as jnp
from jax import lax
from jax.experimental import pallas as pl
from jax.experimental.pallas import tpu as pltpu
from jax.sharding import PartitionSpec as P

HEADS = 8
EPS_NORM = 1e-05
EPS_HEAD = 1e-06
BF = jnp.bfloat16
F32 = jnp.float32
SIDE = 16
SPAN = 128
CHUNKS = 2


def dot(a, b):
    return jnp.dot(a, b, preferred_element_type=F32)


def dot_nt(a, b):
    return lax.dot_general(a, b, (((1,), (1,)), ((), ())), preferred_element_type=F32)


def iota(shape, dim):
    return lax.broadcasted_iota(jnp.int32, shape, dim)


def swap_matrix():
    n = SIDE * SIDE
    r, c = iota((n, n), 0), iota((n, n), 1)
    hit = (r // SIDE == c % SIDE) & (r % SIDE == c // SIDE)
    return jnp.where(hit, 1.0, 0.0).astype(BF)


def head_blocks(head, value):
    n = 4 * head
    same = iota((n, n), 0) // head == iota((n, n), 1) // head
    return jnp.where(same, value, 0.0).astype(BF)


def layer_normalize(x):
    v = x.astype(F32)
    centre = v - jnp.mean(v, axis=-1, keepdims=True)
    spread = jnp.mean(centre * centre, axis=-1, keepdims=True)
    return (centre * lax.rsqrt(spread + EPS_NORM)).astype(BF)


def head_norm(block, averager, eps):
    half = averager.shape[0]
    squares = (block * block).astype(BF)
    out = []
    for c in range(0, block.shape[1], half):
        mean = dot(squares[:, c : c + half], averager)
        out.append((block[:, c : c + half] * lax.rsqrt(mean + eps)).astype(BF))
    return out


def sublayer(x, project_ref, output_ref, line, first=0, count=None):
    tokens, width = x.shape
    count = count or line
    head = width // HEADS
    half = 4 * head
    normed = layer_normalize(x)

    def picked(block):
        if count == line:
            return block
        return block.reshape(tokens // line, line, width)[:, first : first + count].reshape(-1, width)

    queries = head_norm(dot(picked(normed), project_ref[:, :width]), head_blocks(head, 1.0), head * EPS_HEAD)
    keys = head_norm(dot(normed, project_ref[:, width : 2 * width]), head_blocks(head, 1.0 / head), EPS_HEAD)
    values = dot(normed, project_ref[:, 2 * width :]).astype(BF)
    span = SPAN
    asks = span // line * count
    pair = 2 * head
    own = iota((asks, 2 * span), 0) // count == (iota((asks, 2 * span), 1) % span) // line
    left = iota((span, pair), 1) < head
    ones = jnp.where((iota((2 * span, pair), 0) < span) == (iota((2 * span, pair), 1) < head), 1.0, 0.0).astype(BF)

    def spread(block):
        zero = jnp.zeros_like(block)
        return jnp.concatenate([jnp.where(left, block, zero), jnp.where(left, zero, block)], axis=0)

    rows = []
    for i, s in enumerate(range(0, tokens, span)):
        parts = []
        for h in range(0, width, pair):
            c, o = h // half, h % half
            q = queries[c][i * asks : (i + 1) * asks, o : o + pair]
            k = spread(keys[c][s : s + span, o : o + pair])
            v = spread(values[s : s + span, h : h + pair])
            e = jnp.where(own, jnp.exp(dot_nt(q, k)), 0.0).astype(BF)
            r = dot(e, jnp.concatenate([v, ones], axis=1))
            parts.append((r[:, :pair] / r[:, pair:]).astype(BF))
        rows.append(jnp.concatenate(parts, axis=1))
    mixed = jnp.concatenate(rows, axis=0)
    return (picked(x).astype(F32) + dot(mixed, output_ref[...])).astype(BF)


def to_lines(x, swap):
    length, side, width = x.shape
    parts = []
    for a in range(0, length, SIDE):
        tile = x[a : a + SIDE].reshape(SIDE * side, width)
        parts.append(dot(swap, tile).astype(BF).reshape(side, SIDE, width))
    return jnp.concatenate(parts, axis=1).reshape(side * length, width)


def from_lines(x, swap, length):
    width = x.shape[1]
    x = x.reshape(SIDE, length, width)
    parts = []
    for a in range(0, length, SIDE):
        tile = x[:, a : a + SIDE].reshape(SIDE * SIDE, width)
        parts.append(dot(swap, tile).astype(BF).reshape(SIDE, SIDE, width))
    return jnp.concatenate(parts, axis=0)


def feed_forward(x, expand_ref, contract_ref):
    hidden = expand_ref.shape[1]
    piece = 256
    normed = layer_normalize(x)
    total = x.astype(F32)
    for c in range(0, hidden, piece):
        h = jax.nn.gelu(dot(normed, expand_ref[:, c : c + piece])).astype(BF)
        total = total + dot(h, contract_ref[c : c + piece])
    return total.astype(BF)


def like(*shape):
    return jax.ShapeDtypeStruct(shape, BF)


VMEM = pl.BlockSpec(memory_space=pltpu.VMEM)
ANY = pl.BlockSpec(memory_space=pl.ANY)
SMEM = pl.BlockSpec(memory_space=pltpu.SMEM)


def local_call(kernel, out_shape, args, specs, flops, scratch=(), out_spec=VMEM):
    size = sum(a.size * 2 for a in args)
    return pl.pallas_call(
        kernel,
        out_shape=out_shape,
        in_specs=specs,
        out_specs=jax.tree.map(lambda _: out_spec, out_shape),
        scratch_shapes=list(scratch),
        cost_estimate=pl.CostEstimate(flops=flops, bytes_accessed=size, transcendentals=0),
        compiler_params=pltpu.CompilerParams(vmem_limit_bytes=56 * 2**20),
    )(*args)


def column_row_kernel(first, x_hbm, cp_hbm, co_hbm, rp_hbm, ro_hbm, out_hbm, *scratch):
    x_ref, cp_ref, co_ref, rp_ref, ro_ref, mid_ref, out_ref, sems = scratch
    rows, columns, width = x_hbm.shape
    groups = columns // SIDE
    count = out_hbm.shape[0]
    step = math.gcd(count, 512 // columns)

    def at(g):
        return pl.ds(pl.multiple_of(g * SIDE, SIDE), SIDE)

    def fetch(g):
        return pltpu.make_async_copy(x_hbm.at[:, at(g), :], x_ref.at[g], sems.at[g])

    pairs = ((cp_hbm, cp_ref), (co_hbm, co_ref), (rp_hbm, rp_ref), (ro_hbm, ro_ref))
    weights = [pltpu.make_async_copy(h, v, sems.at[groups + i]) for i, (h, v) in enumerate(pairs)]
    fetch(0).start()
    weights[0].start()
    weights[1].start()
    for g in range(1, groups):
        fetch(g).start()
    weights[2].start()
    weights[3].start()
    swap = swap_matrix()
    weights[0].wait()
    weights[1].wait()

    @pl.loop(0, groups)
    def _(g):
        fetch(g).wait()
        y = sublayer(to_lines(x_ref[g], swap), cp_ref, co_ref, rows, first, count)
        mid_ref[:, at(g), :] = from_lines(y, swap, count)

    weights[2].wait()
    weights[3].wait()

    def give(g):
        part = pl.ds(g * step, step)
        return pltpu.make_async_copy(out_ref.at[part], out_hbm.at[part], sems.at[groups + 4])

    @pl.loop(0, count // step)
    def _(g):
        x = mid_ref[pl.ds(g * step, step)].reshape(step * columns, width)
        y = sublayer(x, rp_ref, ro_ref, columns)

        @pl.when(g > 0)
        def _():
            give(g - 1).wait()

        out_ref[pl.ds(g * step, step)] = y.reshape(step, columns, width)
        give(g).start()

    give(count // step - 1).wait()


def frame_lines(x_ref, fp_ref, fo_ref, we_ref, wc_ref, store):
    frames, pixels, _ = x_ref.shape
    swap = swap_matrix()
    size = frames * SIDE
    tiles = math.gcd(pixels // SIDE, max(1, 512 // size))

    @pl.loop(0, pixels // (tiles * SIDE))
    def _(t):
        at = [pl.ds(pl.multiple_of((t * tiles + i) * SIDE, SIDE), SIDE) for i in range(tiles)]
        x = jnp.concatenate([to_lines(x_ref[:, a, :], swap) for a in at], axis=0)
        y = sublayer(x, fp_ref, fo_ref, frames)
        y = feed_forward(y, we_ref, wc_ref)
        for i, a in enumerate(at):
            store(a, from_lines(y[i * size : (i + 1) * size], swap, frames))


def frame_kernel(x_ref, fp_ref, fo_ref, we_ref, wc_ref, *rest):
    out_ref = rest[-1]

    def store(at, z):
        out_ref[:, at, :] = z

    frame_lines(x_ref, fp_ref, fo_ref, we_ref, wc_ref, store)


def frame_sort_kernel(x_ref, fp_ref, fo_ref, we_ref, wc_ref, place_ref, out_ref):
    def store(at, z):
        for f in range(z.shape[0]):
            out_ref[place_ref[f % 2], place_ref[2 + f // 2], at, :] = z[f]

    frame_lines(x_ref, fp_ref, fo_ref, we_ref, wc_ref, store)


def gather_kernel(place_ref, head_ref, own_ref, other_ref, *rest):
    pieces, out_ref, sems = rest[:-2], rest[-2], rest[-1]
    count, size = head_ref.shape[0], own_ref.shape[0]
    copies = [pltpu.make_async_copy(head_ref, out_ref.at[pl.ds(0, count)], sems.at[0])]
    for s in range(len(pieces) + 1):
        for c in range(2):
            owner = 2 * place_ref[2 + s] + place_ref[c]
            to = out_ref.at[pl.ds(pl.multiple_of(count + owner * size, SIDE), size)]
            source = pieces[s - 1].at[c] if s else (own_ref, other_ref)[c]
            copies.append(pltpu.make_async_copy(source, to, sems.at[1 + 2 * s + c]))
    for copy in copies:
        copy.start()
    for copy in copies:
        copy.wait()


def exchange(blocks):
    return lax.all_to_all(blocks, "frame", split_axis=0, concat_axis=0, tiled=True)


def per_device(latent, cp, co, rp, ro, fp, fo, we, wc):
    _, rows, columns, width = latent.shape
    owners = lax.axis_size("frame")
    unit = 2 * columns * width * width
    count = rows // CHUNKS
    chunks = [
        local_call(
            functools.partial(column_row_kernel, first),
            like(count, columns, width),
            (latent[0], cp, co, rp, ro),
            [ANY] * 5,
            unit * (2 * rows + 6 * count),
            [pltpu.VMEM((columns // SIDE, rows, SIDE, width), BF)]
            + [pltpu.VMEM(w.shape, BF) for w in (cp, co, rp, ro)]
            + [pltpu.VMEM((count, columns, width), BF)] * 2
            + [pltpu.SemaphoreType.DMA((columns // SIDE + 5,))],
            ANY,
        )
        for first in range(0, rows, count)
    ]
    share = count * columns // owners
    chips = owners // 2
    me = lax.axis_index("frame")
    chip, core = me // 2, me % 2
    place = jnp.stack([core, 1 - core] + [chip ^ s for s in range(chips)]).astype(jnp.int32)

    def hop(block, step):
        return lax.ppermute(block, "frame", [(i, i ^ step) for i in range(owners)])

    one, two = [exchange(chunk.reshape(owners, share, width)) for chunk in chunks]
    weights = (fp, fo, we, wc)
    one = local_call(
        frame_kernel,
        like(owners, share, width),
        (one, *weights, chunks[1]),
        [VMEM] * 5 + [ANY],
        unit * 12 * count,
    )
    one = exchange(one).reshape(count * columns, width)
    two = local_call(
        frame_sort_kernel,
        like(2, chips, share, width),
        (two, *weights, place),
        [VMEM] * 5 + [SMEM],
        unit * 12 * count,
    )
    other = hop(two[1], 1)
    pieces = [hop(jnp.stack([two[0, s], other[s]]), 2 * s) for s in range(1, chips)]
    result = local_call(
        gather_kernel,
        like(rows * columns, width),
        (place, one, two[0, 0], other[0], *pieces),
        [SMEM] + [VMEM] * (chips + 2),
        unit,
        [pltpu.SemaphoreType.DMA((2 * chips + 1,))],
        ANY,
    )
    return result.reshape(latent.shape)


def solution(mesh):
    placed = (P(("parts", "frame"), None, None, None),) + (P(),) * 8
    return jax.shard_map(
        per_device,
        mesh=mesh,
        in_specs=placed,
        out_specs=P(("parts", "frame"), None, None, None),
        check_vma=False,
    )
```

```python
import functools
import math

import jax
import jax.numpy as jnp
from jax import lax
from jax.experimental import pallas as pl
from jax.experimental.pallas import tpu as pltpu
from jax.sharding import PartitionSpec as P

HEADS = 8
EPS_NORM = 1e-05
EPS_HEAD = 1e-06
BF = jnp.bfloat16
F32 = jnp.float32
SIDE = 16
SPAN = 128
CHUNKS = 2


def dot(a, b):
    return jnp.dot(a, b, preferred_element_type=F32)


def dot_nt(a, b):
    return lax.dot_general(a, b, (((1,), (1,)), ((), ())), preferred_element_type=F32)


def iota(shape, dim):
    return lax.broadcasted_iota(jnp.int32, shape, dim)


def swap_matrix():
    n = SIDE * SIDE
    r, c = iota((n, n), 0), iota((n, n), 1)
    hit = (r // SIDE == c % SIDE) & (r % SIDE == c // SIDE)
    return jnp.where(hit, 1.0, 0.0).astype(BF)


def head_blocks(head, value):
    n = 4 * head
    same = iota((n, n), 0) // head == iota((n, n), 1) // head
    return jnp.where(same, value, 0.0).astype(BF)


def layer_normalize(x):
    v = x.astype(F32)
    centre = v - jnp.mean(v, axis=-1, keepdims=True)
    spread = jnp.mean(centre * centre, axis=-1, keepdims=True)
    return (centre * lax.rsqrt(spread + EPS_NORM)).astype(BF)


def head_norm(block, averager, eps):
    half = averager.shape[0]
    squares = (block * block).astype(BF)
    out = []
    for c in range(0, block.shape[1], half):
        mean = dot(squares[:, c : c + half], averager)
        out.append((block[:, c : c + half] * lax.rsqrt(mean + eps)).astype(BF))
    return out


def sublayer(x, project_ref, output_ref, line, first=0, count=None):
    tokens, width = x.shape
    count = count or line
    head = width // HEADS
    half = 4 * head
    normed = layer_normalize(x)

    def picked(block):
        if count == line:
            return block
        return block.reshape(tokens // line, line, width)[:, first : first + count].reshape(-1, width)

    queries = head_norm(dot(picked(normed), project_ref[:, :width]), head_blocks(head, 1.0), head * EPS_HEAD)
    keys = head_norm(dot(normed, project_ref[:, width : 2 * width]), head_blocks(head, 1.0 / head), EPS_HEAD)
    values = dot(normed, project_ref[:, 2 * width :]).astype(BF)
    span = SPAN
    asks = span // line * count
    pair = 2 * head
    own = iota((asks, 2 * span), 0) // count == (iota((asks, 2 * span), 1) % span) // line
    left = iota((span, pair), 1) < head
    ones = jnp.where((iota((2 * span, pair), 0) < span) == (iota((2 * span, pair), 1) < head), 1.0, 0.0).astype(BF)

    def spread(block):
        zero = jnp.zeros_like(block)
        return jnp.concatenate([jnp.where(left, block, zero), jnp.where(left, zero, block)], axis=0)

    rows = []
    for i, s in enumerate(range(0, tokens, span)):
        parts = []
        for h in range(0, width, pair):
            c, o = h // half, h % half
            q = queries[c][i * asks : (i + 1) * asks, o : o + pair]
            k = spread(keys[c][s : s + span, o : o + pair])
            v = spread(values[s : s + span, h : h + pair])
            e = jnp.where(own, jnp.exp(dot_nt(q, k)), 0.0).astype(BF)
            r = dot(e, jnp.concatenate([v, ones], axis=1))
            parts.append((r[:, :pair] / r[:, pair:]).astype(BF))
        rows.append(jnp.concatenate(parts, axis=1))
    mixed = jnp.concatenate(rows, axis=0)
    return (picked(x).astype(F32) + dot(mixed, output_ref[...])).astype(BF)


def to_lines(x, swap):
    length, side, width = x.shape
    parts = []
    for a in range(0, length, SIDE):
        tile = x[a : a + SIDE].reshape(SIDE * side, width)
        parts.append(dot(swap, tile).astype(BF).reshape(side, SIDE, width))
    return jnp.concatenate(parts, axis=1).reshape(side * length, width)


def from_lines(x, swap, length):
    width = x.shape[1]
    x = x.reshape(SIDE, length, width)
    parts = []
    for a in range(0, length, SIDE):
        tile = x[:, a : a + SIDE].reshape(SIDE * SIDE, width)
        parts.append(dot(swap, tile).astype(BF).reshape(SIDE, SIDE, width))
    return jnp.concatenate(parts, axis=0)


def feed_forward(x, expand_ref, contract_ref):
    hidden = expand_ref.shape[1]
    piece = 256
    normed = layer_normalize(x)
    total = x.astype(F32)
    for c in range(0, hidden, piece):
        h = jax.nn.gelu(dot(normed, expand_ref[:, c : c + piece])).astype(BF)
        total = total + dot(h, contract_ref[c : c + piece])
    return total.astype(BF)


def like(*shape):
    return jax.ShapeDtypeStruct(shape, BF)


VMEM = pl.BlockSpec(memory_space=pltpu.VMEM)
ANY = pl.BlockSpec(memory_space=pl.ANY)
SMEM = pl.BlockSpec(memory_space=pltpu.SMEM)


def local_call(kernel, out_shape, args, specs, flops, scratch=(), out_spec=VMEM, alias=None):
    size = sum(a.size * 2 for a in args)
    return pl.pallas_call(
        kernel,
        out_shape=out_shape,
        in_specs=specs,
        out_specs=jax.tree.map(lambda _: out_spec, out_shape),
        scratch_shapes=list(scratch),
        input_output_aliases=alias or {},
        cost_estimate=pl.CostEstimate(flops=flops, bytes_accessed=size, transcendentals=0),
        compiler_params=pltpu.CompilerParams(vmem_limit_bytes=56 * 2**20),
    )(*args)


def column_row_kernel(first, x_hbm, cp_hbm, co_hbm, rp_hbm, ro_hbm, out_hbm, *scratch):
    x_ref, cp_ref, co_ref, rp_ref, ro_ref, mid_ref, out_ref, sems = scratch
    rows, columns, width = x_hbm.shape
    groups = columns // SIDE
    count = out_hbm.shape[0]
    step = math.gcd(count, 512 // columns)

    def at(g):
        return pl.ds(pl.multiple_of(g * SIDE, SIDE), SIDE)

    def fetch(g):
        return pltpu.make_async_copy(x_hbm.at[:, at(g), :], x_ref.at[g], sems.at[g])

    pairs = ((cp_hbm, cp_ref), (co_hbm, co_ref), (rp_hbm, rp_ref), (ro_hbm, ro_ref))
    weights = [pltpu.make_async_copy(h, v, sems.at[groups + i]) for i, (h, v) in enumerate(pairs)]
    fetch(0).start()
    weights[0].start()
    weights[1].start()
    for g in range(1, groups):
        fetch(g).start()
    weights[2].start()
    weights[3].start()
    swap = swap_matrix()
    weights[0].wait()
    weights[1].wait()

    @pl.loop(0, groups)
    def _(g):
        fetch(g).wait()
        y = sublayer(to_lines(x_ref[g], swap), cp_ref, co_ref, rows, first, count)
        mid_ref[:, at(g), :] = from_lines(y, swap, count)

    weights[2].wait()
    weights[3].wait()

    def give(g):
        part = pl.ds(g * step, step)
        return pltpu.make_async_copy(out_ref.at[part], out_hbm.at[part], sems.at[groups + 4])

    @pl.loop(0, count // step)
    def _(g):
        x = mid_ref[pl.ds(g * step, step)].reshape(step * columns, width)
        y = sublayer(x, rp_ref, ro_ref, columns)

        @pl.when(g > 0)
        def _():
            give(g - 1).wait()

        out_ref[pl.ds(g * step, step)] = y.reshape(step, columns, width)
        give(g).start()

    give(count // step - 1).wait()


def frame_lines(x_ref, fp_ref, fo_ref, we_ref, wc_ref, store):
    frames, pixels, _ = x_ref.shape
    swap = swap_matrix()
    size = frames * SIDE
    tiles = math.gcd(pixels // SIDE, max(1, 512 // size))

    @pl.loop(0, pixels // (tiles * SIDE))
    def _(t):
        at = [pl.ds(pl.multiple_of((t * tiles + i) * SIDE, SIDE), SIDE) for i in range(tiles)]
        x = jnp.concatenate([to_lines(x_ref[:, a, :], swap) for a in at], axis=0)
        y = sublayer(x, fp_ref, fo_ref, frames)
        y = feed_forward(y, we_ref, wc_ref)
        for i, a in enumerate(at):
            store(a, from_lines(y[i * size : (i + 1) * size], swap, frames))


def frame_kernel(x_ref, fp_ref, fo_ref, we_ref, wc_ref, *rest):
    out_ref = rest[-1]

    def store(at, z):
        out_ref[:, at, :] = z

    frame_lines(x_ref, fp_ref, fo_ref, we_ref, wc_ref, store)


def frame_sort_kernel(x_ref, fp_ref, fo_ref, we_ref, wc_ref, place_ref, out_ref):
    def store(at, z):
        for f in range(z.shape[0]):
            out_ref[place_ref[f % 2], place_ref[2 + f // 2], at, :] = z[f]

    frame_lines(x_ref, fp_ref, fo_ref, we_ref, wc_ref, store)


def head_kernel(head_ref, out_ref, sem):
    copy = pltpu.make_async_copy(head_ref, out_ref.at[pl.ds(0, head_ref.shape[0])], sem)
    copy.start()
    copy.wait()


def gather_kernel(count, place_ref, own_ref, other_ref, *rest):
    pieces, out_ref, sems = rest[:-3], rest[-2], rest[-1]
    size = own_ref.shape[0]
    copies = []
    for s in range(len(pieces) + 1):
        for c in range(2):
            owner = 2 * place_ref[2 + s] + place_ref[c]
            to = out_ref.at[pl.ds(pl.multiple_of(count + owner * size, SIDE), size)]
            source = pieces[s - 1].at[c] if s else (own_ref, other_ref)[c]
            copies.append(pltpu.make_async_copy(source, to, sems.at[2 * s + c]))
    for copy in copies:
        copy.start()
    for copy in copies:
        copy.wait()


def exchange(blocks):
    return lax.all_to_all(blocks, "frame", split_axis=0, concat_axis=0, tiled=True)


def per_device(latent, cp, co, rp, ro, fp, fo, we, wc):
    _, rows, columns, width = latent.shape
    owners = lax.axis_size("frame")
    unit = 2 * columns * width * width
    count = rows // CHUNKS
    chunks = [
        local_call(
            functools.partial(column_row_kernel, first),
            like(count, columns, width),
            (latent[0], cp, co, rp, ro),
            [ANY] * 5,
            unit * (2 * rows + 6 * count),
            [pltpu.VMEM((columns // SIDE, rows, SIDE, width), BF)]
            + [pltpu.VMEM(w.shape, BF) for w in (cp, co, rp, ro)]
            + [pltpu.VMEM((count, columns, width), BF)] * 2
            + [pltpu.SemaphoreType.DMA((columns // SIDE + 5,))],
            ANY,
        )
        for first in range(0, rows, count)
    ]
    share = count * columns // owners
    chips = owners // 2
    me = lax.axis_index("frame")
    chip, core = me // 2, me % 2
    place = jnp.stack([core, 1 - core] + [chip ^ s for s in range(chips)]).astype(jnp.int32)

    def hop(block, step):
        return lax.ppermute(block, "frame", [(i, i ^ step) for i in range(owners)])

    one, two = [exchange(chunk.reshape(owners, share, width)) for chunk in chunks]
    weights = (fp, fo, we, wc)
    one = local_call(
        frame_kernel,
        like(owners, share, width),
        (one, *weights, chunks[1]),
        [VMEM] * 5 + [ANY],
        unit * 12 * count,
    )
    one = exchange(one).reshape(count * columns, width)
    two = local_call(
        frame_sort_kernel,
        like(2, chips, share, width),
        (two, *weights, place),
        [VMEM] * 5 + [SMEM],
        unit * 12 * count,
    )
    other = hop(two[1], 1)
    pieces = [hop(jnp.stack([two[0, s], other[s]]), 2 * s) for s in range(1, chips)]
    whole = like(rows * columns, width)
    result = local_call(head_kernel, whole, (one,), [VMEM], unit, [pltpu.SemaphoreType.DMA], ANY)
    result = local_call(
        functools.partial(gather_kernel, count * columns),
        whole,
        (place, two[0, 0], other[0], *pieces, result),
        [SMEM] + [VMEM] * (chips + 1) + [ANY],
        unit,
        [pltpu.SemaphoreType.DMA((2 * chips,))],
        ANY,
        {chips + 2: 0},
    )
    return result.reshape(latent.shape)


def solution(mesh):
    placed = (P(("parts", "frame"), None, None, None),) + (P(),) * 8
    return jax.shard_map(
        per_device,
        mesh=mesh,
        in_specs=placed,
        out_specs=P(("parts", "frame"), None, None, None),
        check_vma=False,
    )
```

```python
import functools
import math

import jax
import jax.numpy as jnp
from jax import lax
from jax.experimental import pallas as pl
from jax.experimental.pallas import tpu as pltpu
from jax.sharding import PartitionSpec as P

HEADS = 8
EPS_NORM = 1e-05
EPS_HEAD = 1e-06
BF = jnp.bfloat16
F32 = jnp.float32
SIDE = 16
SPAN = 128
CHUNKS = 2


def dot(a, b):
    return jnp.dot(a, b, preferred_element_type=F32)


def dot_nt(a, b):
    return lax.dot_general(a, b, (((1,), (1,)), ((), ())), preferred_element_type=F32)


def iota(shape, dim):
    return lax.broadcasted_iota(jnp.int32, shape, dim)


def swap_matrix():
    n = SIDE * SIDE
    r, c = iota((n, n), 0), iota((n, n), 1)
    hit = (r // SIDE == c % SIDE) & (r % SIDE == c // SIDE)
    return jnp.where(hit, 1.0, 0.0).astype(BF)


def head_blocks(head, value):
    n = 4 * head
    same = iota((n, n), 0) // head == iota((n, n), 1) // head
    return jnp.where(same, value, 0.0).astype(BF)


def layer_normalize(x):
    v = x.astype(F32)
    centre = v - jnp.mean(v, axis=-1, keepdims=True)
    spread = jnp.mean(centre * centre, axis=-1, keepdims=True)
    return (centre * lax.rsqrt(spread + EPS_NORM)).astype(BF)


def head_norm(block, averager, eps):
    half = averager.shape[0]
    squares = (block * block).astype(BF)
    out = []
    for c in range(0, block.shape[1], half):
        mean = dot(squares[:, c : c + half], averager)
        out.append((block[:, c : c + half] * lax.rsqrt(mean + eps)).astype(BF))
    return out


def sublayer(x, project_ref, output_ref, line, first=0, count=None):
    tokens, width = x.shape
    count = count or line
    head = width // HEADS
    half = 4 * head
    normed = layer_normalize(x)

    def picked(block):
        if count == line:
            return block
        return block.reshape(tokens // line, line, width)[:, first : first + count].reshape(-1, width)

    queries = head_norm(dot(picked(normed), project_ref[:, :width]), head_blocks(head, 1.0), head * EPS_HEAD)
    keys = head_norm(dot(normed, project_ref[:, width : 2 * width]), head_blocks(head, 1.0 / head), EPS_HEAD)
    values = dot(normed, project_ref[:, 2 * width :]).astype(BF)
    span = SPAN
    asks = span // line * count
    pair = 2 * head
    own = iota((asks, 2 * span), 0) // count == (iota((asks, 2 * span), 1) % span) // line
    left = iota((span, pair), 1) < head
    ones = jnp.where((iota((2 * span, pair), 0) < span) == (iota((2 * span, pair), 1) < head), 1.0, 0.0).astype(BF)

    def spread(block):
        zero = jnp.zeros_like(block)
        return jnp.concatenate([jnp.where(left, block, zero), jnp.where(left, zero, block)], axis=0)

    rows = []
    for i, s in enumerate(range(0, tokens, span)):
        parts = []
        for h in range(0, width, pair):
            c, o = h // half, h % half
            q = queries[c][i * asks : (i + 1) * asks, o : o + pair]
            k = spread(keys[c][s : s + span, o : o + pair])
            v = spread(values[s : s + span, h : h + pair])
            e = jnp.where(own, jnp.exp(dot_nt(q, k)), 0.0).astype(BF)
            r = dot(e, jnp.concatenate([v, ones], axis=1))
            parts.append((r[:, :pair] / r[:, pair:]).astype(BF))
        rows.append(jnp.concatenate(parts, axis=1))
    mixed = jnp.concatenate(rows, axis=0)
    return (picked(x).astype(F32) + dot(mixed, output_ref[...])).astype(BF)


def to_lines(x, swap):
    length, side, width = x.shape
    parts = []
    for a in range(0, length, SIDE):
        tile = x[a : a + SIDE].reshape(SIDE * side, width)
        parts.append(dot(swap, tile).astype(BF).reshape(side, SIDE, width))
    return jnp.concatenate(parts, axis=1).reshape(side * length, width)


def from_lines(x, swap, length):
    width = x.shape[1]
    x = x.reshape(SIDE, length, width)
    parts = []
    for a in range(0, length, SIDE):
        tile = x[:, a : a + SIDE].reshape(SIDE * SIDE, width)
        parts.append(dot(swap, tile).astype(BF).reshape(SIDE, SIDE, width))
    return jnp.concatenate(parts, axis=0)


def feed_forward(x, expand_ref, contract_ref):
    hidden = expand_ref.shape[1]
    piece = 256
    normed = layer_normalize(x)
    total = x.astype(F32)
    for c in range(0, hidden, piece):
        h = jax.nn.gelu(dot(normed, expand_ref[:, c : c + piece])).astype(BF)
        total = total + dot(h, contract_ref[c : c + piece])
    return total.astype(BF)


def like(*shape):
    return jax.ShapeDtypeStruct(shape, BF)


VMEM = pl.BlockSpec(memory_space=pltpu.VMEM)
ANY = pl.BlockSpec(memory_space=pl.ANY)
SMEM = pl.BlockSpec(memory_space=pltpu.SMEM)


def local_call(kernel, out_shape, args, specs, flops, scratch=(), out_spec=VMEM, alias=None):
    size = sum(a.size * 2 for a in args)
    return pl.pallas_call(
        kernel,
        out_shape=out_shape,
        in_specs=specs,
        out_specs=jax.tree.map(lambda _: out_spec, out_shape),
        scratch_shapes=list(scratch),
        input_output_aliases=alias or {},
        cost_estimate=pl.CostEstimate(flops=flops, bytes_accessed=size, transcendentals=0),
        compiler_params=pltpu.CompilerParams(vmem_limit_bytes=56 * 2**20),
    )(*args)


def column_row_kernel(first, x_hbm, cp_hbm, co_hbm, rp_hbm, ro_hbm, out_hbm, *scratch):
    x_ref, cp_ref, co_ref, rp_ref, ro_ref, mid_ref, out_ref, sems = scratch
    rows, columns, width = x_hbm.shape
    groups = columns // SIDE
    count = out_hbm.shape[0]
    step = math.gcd(count, 512 // columns)

    def at(g):
        return pl.ds(pl.multiple_of(g * SIDE, SIDE), SIDE)

    def fetch(g):
        return pltpu.make_async_copy(x_hbm.at[:, at(g), :], x_ref.at[g], sems.at[g])

    pairs = ((cp_hbm, cp_ref), (co_hbm, co_ref), (rp_hbm, rp_ref), (ro_hbm, ro_ref))
    weights = [pltpu.make_async_copy(h, v, sems.at[groups + i]) for i, (h, v) in enumerate(pairs)]
    fetch(0).start()
    weights[0].start()
    weights[1].start()
    for g in range(1, groups):
        fetch(g).start()
    weights[2].start()
    weights[3].start()
    swap = swap_matrix()
    weights[0].wait()
    weights[1].wait()

    @pl.loop(0, groups)
    def _(g):
        fetch(g).wait()
        y = sublayer(to_lines(x_ref[g], swap), cp_ref, co_ref, rows, first, count)
        mid_ref[:, at(g), :] = from_lines(y, swap, count)

    weights[2].wait()
    weights[3].wait()

    def give(g):
        part = pl.ds(g * step, step)
        return pltpu.make_async_copy(out_ref.at[part], out_hbm.at[part], sems.at[groups + 4])

    @pl.loop(0, count // step)
    def _(g):
        x = mid_ref[pl.ds(g * step, step)].reshape(step * columns, width)
        y = sublayer(x, rp_ref, ro_ref, columns)

        @pl.when(g > 0)
        def _():
            give(g - 1).wait()

        out_ref[pl.ds(g * step, step)] = y.reshape(step, columns, width)
        give(g).start()

    give(count // step - 1).wait()


def frame_lines(x_ref, fp_ref, fo_ref, we_ref, wc_ref, store):
    frames, pixels, _ = x_ref.shape
    swap = swap_matrix()
    size = frames * SIDE
    tiles = math.gcd(pixels // SIDE, max(1, 512 // size))

    @pl.loop(0, pixels // (tiles * SIDE))
    def _(t):
        at = [pl.ds(pl.multiple_of((t * tiles + i) * SIDE, SIDE), SIDE) for i in range(tiles)]
        x = jnp.concatenate([to_lines(x_ref[:, a, :], swap) for a in at], axis=0)
        y = sublayer(x, fp_ref, fo_ref, frames)
        y = feed_forward(y, we_ref, wc_ref)
        for i, a in enumerate(at):
            store(a, from_lines(y[i * size : (i + 1) * size], swap, frames))


def frame_kernel(x_ref, fp_ref, fo_ref, we_ref, wc_ref, *rest):
    out_ref = rest[-1]

    def store(at, z):
        out_ref[:, at, :] = z

    frame_lines(x_ref, fp_ref, fo_ref, we_ref, wc_ref, store)


def frame_sort_kernel(x_ref, fp_ref, fo_ref, we_ref, wc_ref, place_ref, own_ref, other_ref):
    first = place_ref[0] == 0

    def store(at, z):
        for f in range(0, z.shape[0], 2):
            step = place_ref[2 + f // 2]
            own_ref[step, at, :] = jnp.where(first, z[f], z[f + 1])
            other_ref[step, at, :] = jnp.where(first, z[f + 1], z[f])

    frame_lines(x_ref, fp_ref, fo_ref, we_ref, wc_ref, store)


def head_kernel(head_ref, out_ref, sem):
    copy = pltpu.make_async_copy(head_ref, out_ref.at[pl.ds(0, head_ref.shape[0])], sem)
    copy.start()
    copy.wait()


def gather_kernel(count, nearest, place_ref, *refs):
    pieces, out_ref, sems = refs[:-3], refs[-2], refs[-1]
    size = pieces[0].shape[1]
    copies = []
    for i, piece in enumerate(pieces):
        for c in range(2):
            owner = 2 * place_ref[2 + nearest + i] + place_ref[c]
            to = out_ref.at[pl.ds(pl.multiple_of(count + owner * size, SIDE), size)]
            copies.append(pltpu.make_async_copy(piece.at[c], to, sems.at[2 * i + c]))
    for copy in copies:
        copy.start()
    for copy in copies:
        copy.wait()


def exchange(blocks):
    return lax.all_to_all(blocks, "frame", split_axis=0, concat_axis=0, tiled=True)


def per_device(latent, cp, co, rp, ro, fp, fo, we, wc):
    _, rows, columns, width = latent.shape
    owners = lax.axis_size("frame")
    unit = 2 * columns * width * width
    count = rows // CHUNKS
    chunks = [
        local_call(
            functools.partial(column_row_kernel, first),
            like(count, columns, width),
            (latent[0], cp, co, rp, ro),
            [ANY] * 5,
            unit * (2 * rows + 6 * count),
            [pltpu.VMEM((columns // SIDE, rows, SIDE, width), BF)]
            + [pltpu.VMEM(w.shape, BF) for w in (cp, co, rp, ro)]
            + [pltpu.VMEM((count, columns, width), BF)] * 2
            + [pltpu.SemaphoreType.DMA((columns // SIDE + 5,))],
            ANY,
        )
        for first in range(0, rows, count)
    ]
    share = count * columns // owners
    chips = owners // 2
    me = lax.axis_index("frame")
    chip, core = me // 2, me % 2
    place = jnp.stack([core, 1 - core] + [chip ^ s for s in range(chips)]).astype(jnp.int32)

    def hop(block, step):
        return lax.ppermute(block, "frame", [(i, i ^ step) for i in range(owners)])

    one, two = [exchange(chunk.reshape(owners, share, width)) for chunk in chunks]
    weights = (fp, fo, we, wc)
    one = local_call(
        frame_kernel,
        like(owners, share, width),
        (one, *weights, chunks[1]),
        [VMEM] * 5 + [ANY],
        unit * 12 * count,
    )
    one = exchange(one).reshape(count * columns, width)
    own, other = local_call(
        frame_sort_kernel,
        [like(chips, share, width)] * 2,
        (two, *weights, place),
        [VMEM] * 5 + [SMEM],
        unit * 12 * count,
    )
    other = hop(other, 1)
    pieces = [jnp.stack([own[s], other[s]]) for s in range(chips)]
    pieces = pieces[:1] + [hop(pieces[s], 2 * s) for s in range(1, chips)]
    whole = like(rows * columns, width)
    result = local_call(head_kernel, whole, (one,), [VMEM], unit, [pltpu.SemaphoreType.DMA], ANY)
    half = chips // 2
    for nearest in (0, half):
        result = local_call(
            functools.partial(gather_kernel, count * columns, nearest),
            whole,
            (place, *pieces[nearest : nearest + half], result),
            [SMEM] + [VMEM] * half + [ANY],
            unit,
            [pltpu.SemaphoreType.DMA((2 * half,))],
            ANY,
            {half + 1: 0},
        )
    return result.reshape(latent.shape)


def solution(mesh):
    placed = (P(("parts", "frame"), None, None, None),) + (P(),) * 8
    return jax.shard_map(
        per_device,
        mesh=mesh,
        in_specs=placed,
        out_specs=P(("parts", "frame"), None, None, None),
        check_vma=False,
    )
```

```python
import functools
import math

import jax
import jax.numpy as jnp
from jax import lax
from jax.experimental import pallas as pl
from jax.experimental.pallas import tpu as pltpu
from jax.sharding import PartitionSpec as P

HEADS = 8
EPS_NORM = 1e-05
EPS_HEAD = 1e-06
BF = jnp.bfloat16
F32 = jnp.float32
SIDE = 16
SPAN = 128
CHUNKS = 2


def dot(a, b):
    return jnp.dot(a, b, preferred_element_type=F32)


def dot_nt(a, b):
    return lax.dot_general(a, b, (((1,), (1,)), ((), ())), preferred_element_type=F32)


def iota(shape, dim):
    return lax.broadcasted_iota(jnp.int32, shape, dim)


def swap_matrix():
    n = SIDE * SIDE
    r, c = iota((n, n), 0), iota((n, n), 1)
    hit = (r // SIDE == c % SIDE) & (r % SIDE == c // SIDE)
    return jnp.where(hit, 1.0, 0.0).astype(BF)


def head_blocks(head, value):
    n = 4 * head
    same = iota((n, n), 0) // head == iota((n, n), 1) // head
    return jnp.where(same, value, 0.0).astype(BF)


def layer_normalize(x):
    v = x.astype(F32)
    centre = v - jnp.mean(v, axis=-1, keepdims=True)
    spread = jnp.mean(centre * centre, axis=-1, keepdims=True)
    return (centre * lax.rsqrt(spread + EPS_NORM)).astype(BF)


def head_norm(block, averager, eps):
    half = averager.shape[0]
    squares = (block * block).astype(BF)
    out = []
    for c in range(0, block.shape[1], half):
        mean = dot(squares[:, c : c + half], averager)
        out.append((block[:, c : c + half] * lax.rsqrt(mean + eps)).astype(BF))
    return out


def sublayer(x, project_ref, output_ref, line, first=0, count=None):
    tokens, width = x.shape
    count = count or line
    head = width // HEADS
    half = 4 * head
    normed = layer_normalize(x)

    def picked(block):
        if count == line:
            return block
        return block.reshape(tokens // line, line, width)[:, first : first + count].reshape(-1, width)

    queries = head_norm(dot(picked(normed), project_ref[:, :width]), head_blocks(head, 1.0), head * EPS_HEAD)
    keys = head_norm(dot(normed, project_ref[:, width : 2 * width]), head_blocks(head, 1.0 / head), EPS_HEAD)
    values = dot(normed, project_ref[:, 2 * width :]).astype(BF)
    span = SPAN
    asks = span // line * count
    pair = 2 * head
    own = iota((asks, 2 * span), 0) // count == (iota((asks, 2 * span), 1) % span) // line
    left = iota((span, pair), 1) < head
    ones = jnp.where((iota((2 * span, pair), 0) < span) == (iota((2 * span, pair), 1) < head), 1.0, 0.0).astype(BF)

    def spread(block):
        zero = jnp.zeros_like(block)
        return jnp.concatenate([jnp.where(left, block, zero), jnp.where(left, zero, block)], axis=0)

    rows = []
    for i, s in enumerate(range(0, tokens, span)):
        parts = []
        for h in range(0, width, pair):
            c, o = h // half, h % half
            q = queries[c][i * asks : (i + 1) * asks, o : o + pair]
            k = spread(keys[c][s : s + span, o : o + pair])
            v = spread(values[s : s + span, h : h + pair])
            e = jnp.where(own, jnp.exp(dot_nt(q, k)), 0.0).astype(BF)
            r = dot(e, jnp.concatenate([v, ones], axis=1))
            parts.append((r[:, :pair] / r[:, pair:]).astype(BF))
        rows.append(jnp.concatenate(parts, axis=1))
    mixed = jnp.concatenate(rows, axis=0)
    return (picked(x).astype(F32) + dot(mixed, output_ref[...])).astype(BF)


def to_lines(x, swap):
    length, side, width = x.shape
    parts = []
    for a in range(0, length, SIDE):
        tile = x[a : a + SIDE].reshape(SIDE * side, width)
        parts.append(dot(swap, tile).astype(BF).reshape(side, SIDE, width))
    return jnp.concatenate(parts, axis=1).reshape(side * length, width)


def from_lines(x, swap, length):
    width = x.shape[1]
    x = x.reshape(SIDE, length, width)
    parts = []
    for a in range(0, length, SIDE):
        tile = x[:, a : a + SIDE].reshape(SIDE * SIDE, width)
        parts.append(dot(swap, tile).astype(BF).reshape(SIDE, SIDE, width))
    return jnp.concatenate(parts, axis=0)


def feed_forward(x, expand_ref, contract_ref):
    hidden = expand_ref.shape[1]
    piece = 256
    normed = layer_normalize(x)
    total = x.astype(F32)
    for c in range(0, hidden, piece):
        h = jax.nn.gelu(dot(normed, expand_ref[:, c : c + piece])).astype(BF)
        total = total + dot(h, contract_ref[c : c + piece])
    return total.astype(BF)


def like(*shape):
    return jax.ShapeDtypeStruct(shape, BF)


VMEM = pl.BlockSpec(memory_space=pltpu.VMEM)
ANY = pl.BlockSpec(memory_space=pl.ANY)
SMEM = pl.BlockSpec(memory_space=pltpu.SMEM)


def local_call(kernel, out_shape, args, specs, flops, scratch=(), out_spec=VMEM, alias=None):
    size = sum(a.size * 2 for a in args)
    return pl.pallas_call(
        kernel,
        out_shape=out_shape,
        in_specs=specs,
        out_specs=jax.tree.map(lambda _: out_spec, out_shape),
        scratch_shapes=list(scratch),
        input_output_aliases=alias or {},
        cost_estimate=pl.CostEstimate(flops=flops, bytes_accessed=size, transcendentals=0),
        compiler_params=pltpu.CompilerParams(vmem_limit_bytes=56 * 2**20),
    )(*args)


def column_row_kernel(first, x_hbm, cp_hbm, co_hbm, rp_hbm, ro_hbm, out_hbm, *scratch):
    x_ref, cp_ref, co_ref, rp_ref, ro_ref, mid_ref, out_ref, sems = scratch
    rows, columns, width = x_hbm.shape
    groups = columns // SIDE
    count = out_hbm.shape[0]
    step = math.gcd(count, 512 // columns)

    def at(g):
        return pl.ds(pl.multiple_of(g * SIDE, SIDE), SIDE)

    def fetch(g):
        return pltpu.make_async_copy(x_hbm.at[:, at(g), :], x_ref.at[g], sems.at[g])

    pairs = ((cp_hbm, cp_ref), (co_hbm, co_ref), (rp_hbm, rp_ref), (ro_hbm, ro_ref))
    weights = [pltpu.make_async_copy(h, v, sems.at[groups + i]) for i, (h, v) in enumerate(pairs)]
    fetch(0).start()
    weights[0].start()
    weights[1].start()
    for g in range(1, groups):
        fetch(g).start()
    weights[2].start()
    weights[3].start()
    swap = swap_matrix()
    weights[0].wait()
    weights[1].wait()

    @pl.loop(0, groups)
    def _(g):
        fetch(g).wait()
        y = sublayer(to_lines(x_ref[g], swap), cp_ref, co_ref, rows, first, count)
        mid_ref[:, at(g), :] = from_lines(y, swap, count)

    weights[2].wait()
    weights[3].wait()

    def give(g):
        part = pl.ds(g * step, step)
        return pltpu.make_async_copy(out_ref.at[part], out_hbm.at[part], sems.at[groups + 4])

    @pl.loop(0, count // step)
    def _(g):
        x = mid_ref[pl.ds(g * step, step)].reshape(step * columns, width)
        y = sublayer(x, rp_ref, ro_ref, columns)

        @pl.when(g > 0)
        def _():
            give(g - 1).wait()

        out_ref[pl.ds(g * step, step)] = y.reshape(step, columns, width)
        give(g).start()

    give(count // step - 1).wait()


def frame_lines(x_ref, fp_ref, fo_ref, we_ref, wc_ref, store):
    frames, pixels, _ = x_ref.shape
    swap = swap_matrix()
    size = frames * SIDE
    tiles = math.gcd(pixels // SIDE, max(1, 512 // size))

    @pl.loop(0, pixels // (tiles * SIDE))
    def _(t):
        at = [pl.ds(pl.multiple_of((t * tiles + i) * SIDE, SIDE), SIDE) for i in range(tiles)]
        x = jnp.concatenate([to_lines(x_ref[:, a, :], swap) for a in at], axis=0)
        y = sublayer(x, fp_ref, fo_ref, frames)
        y = feed_forward(y, we_ref, wc_ref)
        for i, a in enumerate(at):
            store(a, from_lines(y[i * size : (i + 1) * size], swap, frames))


def frame_kernel(x_ref, fp_ref, fo_ref, we_ref, wc_ref, *rest):
    out_ref = rest[-1]

    def store(at, z):
        out_ref[:, at, :] = z

    frame_lines(x_ref, fp_ref, fo_ref, we_ref, wc_ref, store)


def frame_sort_kernel(x_ref, fp_ref, fo_ref, we_ref, wc_ref, place_ref, own_ref, other_ref):
    first = place_ref[0] == 0

    def store(at, z):
        for f in range(0, z.shape[0], 2):
            step = place_ref[2 + f // 2]
            own_ref[step, at, :] = jnp.where(first, z[f], z[f + 1])
            other_ref[step, at, :] = jnp.where(first, z[f + 1], z[f])

    frame_lines(x_ref, fp_ref, fo_ref, we_ref, wc_ref, store)


def head_kernel(head_ref, out_ref, sem):
    copy = pltpu.make_async_copy(head_ref, out_ref.at[pl.ds(0, head_ref.shape[0])], sem)
    copy.start()
    copy.wait()


def gather_kernel(count, place_ref, own_ref, other_ref, *rest):
    pieces, out_ref, sems = rest[:-3], rest[-2], rest[-1]
    size = own_ref.shape[0]
    copies = []
    for s in range(len(pieces) + 1):
        for c in range(2):
            owner = 2 * place_ref[2 + s] + place_ref[c]
            to = out_ref.at[pl.ds(pl.multiple_of(count + owner * size, SIDE), size)]
            source = pieces[s - 1].at[c] if s else (own_ref, other_ref)[c]
            copies.append(pltpu.make_async_copy(source, to, sems.at[2 * s + c]))
    for copy in copies:
        copy.start()
    for copy in copies:
        copy.wait()


def exchange(blocks):
    return lax.all_to_all(blocks, "frame", split_axis=0, concat_axis=0, tiled=True)


def per_device(latent, cp, co, rp, ro, fp, fo, we, wc):
    _, rows, columns, width = latent.shape
    owners = lax.axis_size("frame")
    unit = 2 * columns * width * width
    count = rows // CHUNKS
    chunks = [
        local_call(
            functools.partial(column_row_kernel, first),
            like(count, columns, width),
            (latent[0], cp, co, rp, ro),
            [ANY] * 5,
            unit * (2 * rows + 6 * count),
            [pltpu.VMEM((columns // SIDE, rows, SIDE, width), BF)]
            + [pltpu.VMEM(w.shape, BF) for w in (cp, co, rp, ro)]
            + [pltpu.VMEM((count, columns, width), BF)] * 2
            + [pltpu.SemaphoreType.DMA((columns // SIDE + 5,))],
            ANY,
        )
        for first in range(0, rows, count)
    ]
    share = count * columns // owners
    chips = owners // 2
    me = lax.axis_index("frame")
    chip, core = me // 2, me % 2
    place = jnp.stack([core, 1 - core] + [chip ^ s for s in range(chips)]).astype(jnp.int32)

    def hop(block, step):
        return lax.ppermute(block, "frame", [(i, i ^ step) for i in range(owners)])

    one, two = [exchange(chunk.reshape(owners, share, width)) for chunk in chunks]
    weights = (fp, fo, we, wc)
    one = local_call(
        frame_kernel,
        like(owners, share, width),
        (one, *weights, chunks[1]),
        [VMEM] * 5 + [ANY],
        unit * 12 * count,
    )
    one = exchange(one).reshape(count * columns, width)
    own, other = local_call(
        frame_sort_kernel,
        [like(chips, share, width)] * 2,
        (two, *weights, place),
        [VMEM] * 5 + [SMEM],
        unit * 12 * count,
    )
    other = hop(other, 1)
    pieces = [hop(jnp.stack([own[s], other[s]]), 2 * s) for s in range(1, chips)]
    whole = like(rows * columns, width)
    result = local_call(head_kernel, whole, (one,), [VMEM], unit, [pltpu.SemaphoreType.DMA], ANY)
    result = local_call(
        functools.partial(gather_kernel, count * columns),
        whole,
        (place, own[0], other[0], *pieces, result),
        [SMEM] + [VMEM] * (chips + 1) + [ANY],
        unit,
        [pltpu.SemaphoreType.DMA((2 * chips,))],
        ANY,
        {chips + 2: 0},
    )
    return result.reshape(latent.shape)


def solution(mesh):
    placed = (P(("parts", "frame"), None, None, None),) + (P(),) * 8
    return jax.shard_map(
        per_device,
        mesh=mesh,
        in_specs=placed,
        out_specs=P(("parts", "frame"), None, None, None),
        check_vma=False,
    )
```
